32 devices in a mesh: ctx: 8 (over y, x, core), tp: 4 (over z).
Axes of the slice: x: 2, y: 2, z: 4, core: 2. Of those that a mesh axis runs over, the one named last changes fastest.
Arguments:
- hyena_query: bfloat16 [3072, 8192], P('ctx', 'tp'), may hold values from -6 to 6
- hyena_key: bfloat16 [3072, 8192], P('ctx', 'tp'), may hold values from -6 to 6
- hyena_value: bfloat16 [3072, 8192], P('ctx', 'tp'), may hold values from -6 to 6
- conv_filter: bfloat16 [512, 128], P('tp'), may hold values from -0.5 to 0.5
- skip_gain: float32 [8192], P('tp'), may hold values from -4 to 4
- query_rows: bfloat16 [3072, 8192], P('ctx', 'tp'), may hold values from -80 to 80
- key_rows: bfloat16 [3072, 8192], P('ctx', 'tp'), may hold values from -4 to 4, as said below
- value_rows: bfloat16 [3072, 8192], P('ctx', 'tp'), may hold values from -6 to 6
- out_weight: bfloat16 [8192, 8192], P(None, 'tp'), may hold values from -1 to 1
Outputs:
- hyena_out: bfloat16 [3072, 8192], P('ctx', 'tp')
- attention_out: bfloat16 [8192, 3072], P('tp', 'ctx')
The draws below stay inside these ranges and needn't reach their ends.
Inputs may be any that keep to these rules, and one draw needn't show every extreme that they name: `key_rows`: keys of order one.
All inputs are finite; a program needn't handle non-finite values.
Results may differ from the reference program's by a relative error of at most 0.014.
Values may be sent and summed in bfloat16 or wider, within the bound.
A program may use at most 128 MiB of HBM per device.

```python
import jax
import jax.numpy as jnp
import numpy as np
from jax import lax

D = 8192
HEADS = 64
HEAD_DIM = 128
FILTER_LEN = 128
SEQ_LEN = 3072
GROUPS = 512
N_TP = 4


def paired_rows(key):
    base = jax.random.fold_in(key, 11)
    first_key, second_key = jax.random.split(base, 2)
    keys_drawn = jnp.clip(jax.random.normal(first_key, (SEQ_LEN, D), jnp.float32), -4.0, 4.0)
    queries_drawn = jnp.clip(jax.random.normal(second_key, (SEQ_LEN, D), jnp.float32), -4.0, 4.0)
    return (queries_drawn, keys_drawn)


def draw_query_rows(key, part):
    return paired_rows(key)[0].astype(jnp.bfloat16)


def draw_key_rows(key, part):
    return paired_rows(key)[1].astype(jnp.bfloat16)


def with_spikes(array, own_key, source, target, blocks, factor):
    owner, partner = [(jnp.arange(array.shape[dim]) // (array.shape[dim] // blocks)).reshape([-1 if axis == dim else 1 for axis in range(array.ndim)]) for dim in (source, target)]
    chosen = jax.random.permutation(own_key, blocks)[partner]
    strong = (owner == chosen) | (owner == (partner + blocks // 2) % blocks)
    return jnp.where(strong, factor * array, array)


def block_scale(key, shape, cuts, low, top_value):
    level = 1.0
    for axis_at, parts in cuts:
        heights = jax.random.uniform(jax.random.fold_in(jax.random.fold_in(key, 6), axis_at), (parts,), jnp.float32, low / len(cuts), top_value / len(cuts))
        level = level * jnp.repeat(jnp.exp(heights), shape[axis_at] // parts).reshape((-1,) + (1,) * (len(shape) - 1 - axis_at))
    return level


def scatter_about(stream_key, extent, spread, limit, cuts=(), kind=jnp.bfloat16):
    values = spread * jax.random.normal(stream_key, extent, jnp.float32)
    if cuts:
        values = values * block_scale(stream_key, extent, cuts, -0.22, 0.18)
    return jnp.clip(values, -limit, limit).astype(kind)


def noise_with(rng, dims, deviation, bound, cuts, heavy, held_as=jnp.bfloat16):
    values = deviation * jax.random.normal(rng, dims, jnp.float32)
    if cuts:
        values = values * block_scale(rng, dims, cuts, -0.22, 0.18)
    return jnp.clip(with_spikes(values, jax.random.fold_in(rng, 3), *heavy), -bound, bound).astype(held_as)


def setup_inputs(seed: int = 0) -> dict:
    arg_keys = jax.random.split(jax.random.key(seed), 10)
    return {
        "hyena_query": scatter_about(arg_keys[0], (SEQ_LEN, D), 1.0, 6.0, ((0, 8), (1, 4))),
        "hyena_key": scatter_about(arg_keys[1], (SEQ_LEN, D), 1.0, 6.0, ((0, 8), (1, 4))),
        "hyena_value": scatter_about(arg_keys[2], (SEQ_LEN, D), 1.0, 6.0, ((0, 8), (1, 4))),
        "conv_filter": scatter_about(arg_keys[3], (GROUPS, FILTER_LEN), FILTER_LEN ** -0.5, 0.5, ((0, 4),)),
        "skip_gain": scatter_about(arg_keys[4], (D,), 1.0, 4.0, ((0, 4),), jnp.float32),
        "query_rows": draw_query_rows(jax.random.fold_in(arg_keys[9], 71), 0),
        "key_rows": draw_key_rows(jax.random.fold_in(arg_keys[9], 71), 0),
        "value_rows": scatter_about(arg_keys[7], (SEQ_LEN, D), 1.0, 6.0, ((0, 8), (1, 4))),
        "out_weight": noise_with(arg_keys[8], (D, D), HEADS ** -0.5, 1.0, ((1, 4),), (1, 0, 4, 2.0)),
    }


top_precision = lax.Precision.HIGHEST


def toeplitz_pair(filters):
    length = filters.shape[1]
    lag_table = np.arange(length)[:, None] - np.arange(length)[None, :]
    inner_index = np.clip(lag_table, 0, length - 1)
    outer_index = np.clip(lag_table + length, 0, length - 1)
    inner_part = jnp.where(jnp.asarray(lag_table >= 0)[None], filters[:, inner_index], jnp.zeros((), filters.dtype))
    outer_part = jnp.where(jnp.asarray(lag_table < 0)[None], filters[:, outer_index], jnp.zeros((), filters.dtype))
    return inner_part, outer_part


def grouped_conv(current, before, filters):
    blocks, length, feature_width = current.shape
    groups = filters.shape[0]
    inner_part, outer_part = toeplitz_pair(filters)
    inner_part = inner_part.astype(jnp.float32)
    outer_part = outer_part.astype(jnp.float32)
    split_shape = (blocks, length, groups, feature_width // groups)
    result = jnp.einsum("gts,bsgc->btgc", inner_part, current.reshape(split_shape), precision=top_precision)
    result = result + jnp.einsum("gts,bsgc->btgc", outer_part, before.reshape(split_shape), precision=top_precision)
    return result.reshape(blocks * length, feature_width)


def reference(hyena_query, hyena_key, hyena_value, conv_filter, skip_gain, query_rows, key_rows, value_rows, out_weight):
    product = (hyena_key.astype(jnp.float32) * hyena_value.astype(jnp.float32)).astype(jnp.bfloat16)
    widened = lax.optimization_barrier(product).astype(jnp.float32)
    blocks = SEQ_LEN // FILTER_LEN
    current = widened.reshape(blocks, FILTER_LEN, D)
    before = jnp.concatenate([jnp.zeros_like(current[:1]), current[:-1]], axis=0)
    convolved = grouped_conv(current, before, conv_filter)
    hyena_out = (hyena_query.astype(jnp.float32) * (convolved + skip_gain[None, :] * widened)).astype(jnp.bfloat16)

    score_scale = HEAD_DIM ** -0.5
    positions = jnp.arange(SEQ_LEN, dtype=jnp.int32)
    allowed = positions[None, :] <= positions[:, None]

    def one_head(head_index):
        first_col = head_index * HEAD_DIM
        query_part = lax.dynamic_slice_in_dim(query_rows, first_col, HEAD_DIM, 1).astype(jnp.float32)
        key_part = lax.dynamic_slice_in_dim(key_rows, first_col, HEAD_DIM, 1).astype(jnp.float32)
        value_part = lax.dynamic_slice_in_dim(value_rows, first_col, HEAD_DIM, 1).astype(jnp.float32)
        scores = jnp.dot(query_part, key_part.T, precision=top_precision) * score_scale
        scores = jnp.where(allowed, scores, -jnp.inf)
        row_top = jnp.max(scores, axis=1, keepdims=True)
        weights = jnp.exp(scores - row_top)
        row_total = jnp.sum(weights, axis=1, keepdims=True)
        probs = lax.optimization_barrier(weights.astype(jnp.bfloat16)).astype(jnp.float32)
        mixed_rows = jnp.dot(probs, value_part, precision=top_precision)
        return (mixed_rows / row_total).astype(jnp.bfloat16)

    per_head = lax.map(one_head, jnp.arange(HEADS, dtype=jnp.int32))
    attended = jnp.transpose(per_head, (1, 0, 2)).reshape(SEQ_LEN, D)

    group_share = D // N_TP
    attention_out = jnp.zeros((D, SEQ_LEN), jnp.float32)
    for group_index in range(N_TP):
        weight_part = out_weight[:, group_index * group_share:(group_index + 1) * group_share].astype(jnp.float32)
        rows_part = attended[:, group_index * group_share:(group_index + 1) * group_share].astype(jnp.float32)
        partial_sum = jnp.dot(weight_part, rows_part.T, precision=top_precision)
        rounded = lax.optimization_barrier(partial_sum.astype(jnp.bfloat16))
        attention_out = attention_out + rounded.astype(jnp.float32)
    return hyena_out, attention_out.astype(jnp.bfloat16)
```

```python
import functools

import jax
import jax.numpy as jnp
from jax import lax
from jax.experimental import pallas as pl
from jax.experimental.pallas import tpu as pltpu
from jax.sharding import PartitionSpec as P

HEAD_DIM = 128
FIRST_ROWS = 128
EXP_SCALE = HEAD_DIM ** (-0.5) * 1.4426950408889634
MESH = pl.DeviceIdType.MESH
ANY = pl.BlockSpec(memory_space=pl.ANY)


def greet(count, me):
    barrier = pltpu.get_barrier_semaphore()
    for offset in range(1, count):
        peer = lax.rem(me + offset, count)
        pl.semaphore_signal(barrier, inc=1, device_id={"ctx": peer}, device_id_type=MESH)
    pl.semaphore_wait(barrier, count - 1)


def attend(queries, keys, values, known, column):
    rows = queries.shape[0]
    contract = (((1,), (1,)), ((), ()))
    diagonal = keys[pl.ds(known, rows), pl.ds(column, HEAD_DIM)]
    scores = lax.dot_general(queries, diagonal, contract, preferred_element_type=jnp.float32)
    allowed = lax.broadcasted_iota(jnp.int32, (rows, rows), 1) <= lax.broadcasted_iota(
        jnp.int32, (rows, rows), 0
    )
    scores = jnp.where(allowed, scores, -jnp.inf)
    top = jnp.max(scores, axis=1, keepdims=True)
    if known:
        early = lax.dot_general(
            queries,
            keys[pl.ds(0, known), pl.ds(column, HEAD_DIM)],
            contract,
            preferred_element_type=jnp.float32,
        )
        top = jnp.maximum(top, jnp.max(early, axis=1, keepdims=True))
    weights = jnp.exp2((scores - top) * EXP_SCALE)
    total = jnp.sum(weights, axis=1, keepdims=True)
    mixed = jnp.dot(
        weights.astype(jnp.bfloat16),
        values[pl.ds(known, rows), pl.ds(column, HEAD_DIM)],
        preferred_element_type=jnp.float32,
    )
    if known:
        weights = jnp.exp2((early - top) * EXP_SCALE)
        total = total + jnp.sum(weights, axis=1, keepdims=True)
        mixed = mixed + jnp.dot(
            weights.astype(jnp.bfloat16),
            values[pl.ds(0, known), pl.ds(column, HEAD_DIM)],
            preferred_element_type=jnp.float32,
        )
    return (mixed / total).astype(jnp.bfloat16)


def give_back(block, me, width, done, attended, send_sem, recv_sem, local_sem):
    column = pl.multiple_of(me * width, width)
    target = attended.at[:, pl.ds(column, width)]

    @pl.when(me != block)
    def _():
        pltpu.make_async_remote_copy(
            src_ref=done.at[block],
            dst_ref=target,
            send_sem=send_sem.at[block],
            recv_sem=recv_sem.at[me],
            device_id={"ctx": block},
            device_id_type=MESH,
        ).start()

    @pl.when(me == block)
    def _():
        pltpu.make_async_copy(done.at[block], target, local_sem).start()


def end_back(count, me, width, done, attended, send_sem, recv_sem, local_sem):
    for block in range(count):
        column = block * width
        target = attended.at[:, pl.ds(column, width)]

        @pl.when(me != block)
        def _():
            copy = pltpu.make_async_remote_copy(
                src_ref=done.at[block],
                dst_ref=target,
                send_sem=send_sem.at[block],
                recv_sem=recv_sem.at[block],
                device_id={"ctx": block},
                device_id_type=MESH,
            )
            copy.wait_send()
            copy.wait_recv()

        @pl.when(me == block)
        def _():
            pltpu.make_async_copy(done.at[block], target, local_sem).wait()


def first_kernel(
    count,
    query,
    key,
    value,
    attended,
    key_out,
    value_out,
    late_out,
    keys,
    values,
    early,
    done,
    send_sem,
    recv_sem,
    own_sem,
    back_send,
    back_recv,
    back_local,
    out_sem,
):
    me = lax.axis_index("ctx")
    tokens = key.shape[0]
    width = key.shape[1] // count
    first = early.shape[1]
    late = tokens - first

    def pieces(source, reader):
        column = pl.multiple_of(reader * width, width)
        columns = pl.ds(column, width)
        rows = pl.ds(pl.multiple_of(source * tokens, tokens), tokens)
        return (
            (key.at[:, columns], keys.at[rows]),
            (value.at[:, columns], values.at[rows]),
            (query.at[pl.ds(0, first), columns], early.at[source]),
            (query.at[pl.ds(first, late), columns], late_out.at[source]),
        )

    def sent(kind, source, reader, other):
        origin, target = pieces(source, reader)[kind]
        return pltpu.make_async_remote_copy(
            src_ref=origin,
            dst_ref=target,
            send_sem=send_sem.at[kind, reader],
            recv_sem=recv_sem.at[kind, source],
            device_id={"ctx": other},
            device_id_type=MESH,
        )

    def own(kind):
        origin, target = pieces(me, me)[kind]
        return pltpu.make_async_copy(origin, target, own_sem.at[kind])

    greet(count, me)
    for kind in range(4):
        for offset in range(1, count):
            peer = lax.rem(me + offset, count)
            sent(kind, me, peer, peer).start()
        own(kind).start()
    for block in range(count):

        @pl.when(me != block)
        def _():
            for kind in range(3):
                sent(kind, block, me, block).wait_recv()

        @pl.when(me == block)
        def _():
            for kind in range(3):
                own(kind).wait()

        @pl.loop(0, width // HEAD_DIM)
        def _(head):
            column = pl.multiple_of(head * HEAD_DIM, HEAD_DIM)
            done[block, :, pl.ds(column, HEAD_DIM)] = attend(
                early[block, :, pl.ds(column, HEAD_DIM)], keys, values, block * tokens, column
            )

        give_back(block, me, width, done, attended, back_send, back_recv, back_local)
    saved = (
        pltpu.make_async_copy(keys, key_out, out_sem.at[0]),
        pltpu.make_async_copy(values, value_out, out_sem.at[1]),
    )
    for copy in saved:
        copy.start()
    end_back(count, me, width, done, attended, back_send, back_recv, back_local)
    for offset in range(1, count):
        peer = lax.rem(me + offset, count)
        sent(3, peer, me, peer).wait_recv()
        for kind in range(4):
            sent(kind, me, peer, peer).wait_send()
    own(3).wait()
    for copy in saved:
        copy.wait()


def later_kernel(
    count, query, keys, values, attended, done, back_send, back_recv, back_local
):
    me = lax.axis_index("ctx")
    width = keys.shape[1]
    tokens = keys.shape[0] // count
    late = query.shape[1]
    greet(count, me)
    for block in range(count):
        for start in range(0, late, FIRST_ROWS):

            @pl.loop(0, width // HEAD_DIM)
            def _(head):
                column = pl.multiple_of(head * HEAD_DIM, HEAD_DIM)
                columns = pl.ds(column, HEAD_DIM)
                rows = pl.ds(start, FIRST_ROWS)
                known = block * tokens + (tokens - late) + start
                done[block, rows, columns] = attend(
                    query[block, rows, columns], keys, values, known, column
                )

        give_back(block, me, width, done, attended, back_send, back_recv, back_local)
    end_back(count, me, width, done, attended, back_send, back_recv, back_local)


def first_attention(query, key, value, count):
    tokens, features = key.shape
    width = features // count
    late = tokens - FIRST_ROWS
    kind = jnp.bfloat16
    return pl.pallas_call(
        functools.partial(first_kernel, count),
        out_shape=(
            jax.ShapeDtypeStruct((FIRST_ROWS, features), kind),
            jax.ShapeDtypeStruct((count * tokens, width), kind),
            jax.ShapeDtypeStruct((count * tokens, width), kind),
            jax.ShapeDtypeStruct((count, late, width), kind),
        ),
        in_specs=[ANY] * 3,
        out_specs=(ANY,) * 4,
        scratch_shapes=[
            pltpu.VMEM((count * tokens, width), kind),
            pltpu.VMEM((count * tokens, width), kind),
            pltpu.VMEM((count, FIRST_ROWS, width), kind),
            pltpu.VMEM((count, FIRST_ROWS, width), kind),
            pltpu.SemaphoreType.DMA((4, count)),
            pltpu.SemaphoreType.DMA((4, count)),
            pltpu.SemaphoreType.DMA((4,)),
            pltpu.SemaphoreType.DMA((count,)),
            pltpu.SemaphoreType.DMA((count,)),
            pltpu.SemaphoreType.DMA,
            pltpu.SemaphoreType.DMA((2,)),
        ],
        compiler_params=pltpu.CompilerParams(
            collective_id=0, has_side_effects=True, vmem_limit_bytes=40 << 20
        ),
    )(query, key, value)


def later_attention(query, keys, values):
    count, late, width = query.shape
    kind = jnp.bfloat16
    return pl.pallas_call(
        functools.partial(later_kernel, count),
        out_shape=jax.ShapeDtypeStruct((late, count * width), kind),
        in_specs=[pl.BlockSpec(memory_space=pltpu.VMEM)] * 3,
        out_specs=ANY,
        scratch_shapes=[
            pltpu.VMEM((count, late, width), kind),
            pltpu.SemaphoreType.DMA((count,)),
            pltpu.SemaphoreType.DMA((count,)),
            pltpu.SemaphoreType.DMA,
        ],
        compiler_params=pltpu.CompilerParams(
            collective_id=1, has_side_effects=True, vmem_limit_bytes=40 << 20
        ),
    )(query, keys, values)


def project_kernel(weight, attended, out):
    out[...] = lax.dot_general(
        weight[...],
        attended[...],
        (((1,), (1,)), ((), ())),
        preferred_element_type=jnp.float32,
    ).astype(out.dtype)


def project(weight, attended):
    outs, features = weight.shape
    tokens = attended.shape[0]
    step = 512
    return pl.pallas_call(
        project_kernel,
        grid=(outs // step,),
        out_shape=jax.ShapeDtypeStruct((outs, tokens), jnp.bfloat16),
        in_specs=[
            pl.BlockSpec((step, features), lambda i: (i, 0)),
            pl.BlockSpec((tokens, features), lambda i: (0, 0)),
        ],
        out_specs=pl.BlockSpec((step, tokens), lambda i: (i, 0)),
        compiler_params=pltpu.CompilerParams(vmem_limit_bytes=40 << 20),
        cost_estimate=pl.CostEstimate(
            flops=2 * outs * tokens * features,
            bytes_accessed=2 * outs * features,
            transcendentals=0,
        ),
    )(weight, attended)


def summed(partial):
    return lax.psum_scatter(partial, "tp", scatter_dimension=0, tiled=True)


def shifted(block, axis, distance):
    devices = range(lax.axis_size(axis))
    route = [(i - distance, i) for i in devices if i - distance in devices]
    return lax.ppermute(block, axis, route)


def swapped(block, axis, stride):
    count = lax.axis_size(axis)
    route = []
    for low in range(count):
        high = low | 1 << stride
        if high != low and high < count:
            route += [(low, high), (high, low)]
    return lax.ppermute(block, axis, route)


def toeplitz_pair(filters):
    length = filters.shape[1]
    lag_table = (
        jnp.arange(length, dtype=jnp.int32)[:, None] - jnp.arange(length, dtype=jnp.int32)[None, :]
    )
    taps = jnp.arange(length, dtype=jnp.int32)[:, None, None]
    inner_table = (lag_table[None] == taps).astype(jnp.bfloat16)
    outer_table = (lag_table[None] + length == taps).astype(jnp.bfloat16)
    inner_part = jnp.einsum(
        "gj,jts->gts", filters, inner_table, preferred_element_type=jnp.float32
    ).astype(jnp.bfloat16)
    outer_part = jnp.einsum(
        "gj,jts->gts", filters, outer_table, preferred_element_type=jnp.float32
    ).astype(jnp.bfloat16)
    return (inner_part, outer_part)


def local_conv(current, before, filters):
    blocks, length, feature_width = current.shape
    groups = filters.shape[0]
    split_shape = (blocks, length, groups, feature_width // groups)
    inner_part, outer_part = toeplitz_pair(filters)
    result = jnp.einsum(
        "gts,bsgc->btgc",
        inner_part,
        current.reshape(split_shape),
        preferred_element_type=jnp.float32,
    )
    result = result + jnp.einsum(
        "gts,bsgc->btgc",
        outer_part,
        before.reshape(split_shape),
        preferred_element_type=jnp.float32,
    )
    return result.reshape(blocks * length, feature_width)


def half_update(partial_value, block_keys, block_values, block_first, queries, positions):
    row_top, row_total, weighted = partial_value
    score_scale = HEAD_DIM ** (-0.5)
    scores = (
        jnp.einsum("qhd,khd->hqk", queries, block_keys, preferred_element_type=jnp.float32)
        * score_scale
    )
    key_positions = block_first + jnp.arange(block_keys.shape[0], dtype=jnp.int32)
    allowed = key_positions[None, :] <= positions[:, None]
    scores = jnp.where(allowed[None], scores, -jnp.inf)
    new_top = jnp.maximum(row_top, jnp.max(scores, axis=2))
    safe_top = jnp.where(new_top == -jnp.inf, 0.0, new_top)
    keep_factor = jnp.exp(row_top - safe_top)
    weights = jnp.exp(scores - safe_top[:, :, None])
    row_total = row_total * keep_factor + jnp.sum(weights, axis=2)
    weighted = weighted * keep_factor[:, :, None] + jnp.einsum(
        "hqk,khd->hqd",
        weights.astype(jnp.bfloat16),
        block_values,
        preferred_element_type=jnp.float32,
    )
    return (new_top, row_total, weighted)


def hyena(hyena_query, hyena_key, hyena_value, conv_filter, skip_gain):
    product = (hyena_key.astype(jnp.float32) * hyena_value.astype(jnp.float32)).astype(jnp.bfloat16)
    length = conv_filter.shape[1]
    tokens_here, feature_width = product.shape
    blocks = tokens_here // length
    previous = shifted(product[tokens_here - length :], "ctx", 1)
    widened = product.astype(jnp.float32)
    earlier = jnp.concatenate([previous, product[: tokens_here - length]], axis=0)
    convolved = local_conv(
        product.reshape(blocks, length, feature_width),
        earlier.reshape(blocks, length, feature_width),
        conv_filter,
    )
    hyena_out = (
        hyena_query.astype(jnp.float32) * (convolved + skip_gain[None, :] * widened)
    ).astype(jnp.bfloat16)
    return hyena_out


def gathered_attention(query_rows, key_rows, value_rows, out_weight):
    tokens_here, feature_width = key_rows.shape
    ctx_count = lax.axis_size("ctx")
    ctx_index = lax.axis_index("ctx")
    half_rows = tokens_here // 2
    heads_here = feature_width // HEAD_DIM
    offsets = jnp.arange(half_rows, dtype=jnp.int32)
    first_positions = ctx_index * tokens_here + offsets
    second_queries = query_rows[half_rows:]
    for bit_index in range(ctx_count.bit_length() - 1):
        second_queries = swapped(second_queries, "ctx", bit_index)
    second_positions = (ctx_count - 1 - ctx_index) * tokens_here + half_rows + offsets
    query_halves = (
        query_rows[:half_rows].reshape(half_rows, heads_here, HEAD_DIM),
        second_queries.reshape(half_rows, heads_here, HEAD_DIM),
    )
    position_halves = (first_positions, second_positions)
    empty_top = jnp.full((heads_here, half_rows), -jnp.inf, jnp.float32)
    empty_total = jnp.zeros((heads_here, half_rows), jnp.float32)
    empty_weighted = jnp.zeros((heads_here, half_rows, HEAD_DIM), jnp.float32)
    start_state = (
        (empty_top, empty_total, empty_weighted),
        (empty_top, empty_total, empty_weighted),
    )
    key_piece = lax.all_gather(key_rows, "ctx", axis=0, tiled=True)
    value_piece = lax.all_gather(value_rows, "ctx", axis=0, tiled=True)
    piece_rows = key_piece.shape[0]
    step_rows = min(piece_rows, tokens_here)
    count_steps = piece_rows // step_rows
    key_steps = key_piece.reshape(count_steps, step_rows, heads_here, HEAD_DIM)
    value_steps = value_piece.reshape(count_steps, step_rows, heads_here, HEAD_DIM)

    def one_step(carried, inputs):
        block_keys, block_values, step_index = inputs
        block_first = step_index * step_rows
        updated = []
        for half_index in range(2):
            queries = query_halves[half_index]
            positions = position_halves[half_index]

            def apply_update(partial_value, queries=queries, positions=positions):
                return half_update(
                    partial_value, block_keys, block_values, block_first, queries, positions
                )

            def leave_alone(partial_value):
                return partial_value

            updated.append(
                lax.cond(
                    block_first <= positions[half_rows - 1],
                    apply_update,
                    leave_alone,
                    carried[half_index],
                )
            )
        return ((updated[0], updated[1]), None)

    final_state, unused = lax.scan(
        one_step, start_state, (key_steps, value_steps, jnp.arange(count_steps, dtype=jnp.int32))
    )
    first_state, second_state = final_state

    def finish(partial_value):
        row_top, row_total, weighted = partial_value
        normalized = weighted / row_total[:, :, None]
        return (
            jnp.transpose(normalized, (1, 0, 2))
            .reshape(half_rows, feature_width)
            .astype(jnp.bfloat16)
        )

    first_result = finish(first_state)
    second_result = finish(second_state)
    for bit_index in range(ctx_count.bit_length() - 1):
        second_result = swapped(second_result, "ctx", bit_index)
    attended = jnp.concatenate([first_result, second_result], axis=0)
    attention_out = lax.psum_scatter(
        lax.dot_general(
            out_weight, attended, (((1,), (1,)), ((), ())), preferred_element_type=jnp.float32
        ).astype(jnp.bfloat16),
        "tp",
        scatter_dimension=0,
        tiled=True,
    )
    return attention_out


def local(
    hyena_query,
    hyena_key,
    hyena_value,
    conv_filter,
    skip_gain,
    query_rows,
    key_rows,
    value_rows,
    out_weight,
):
    count = lax.axis_size("ctx")
    tokens, features = key_rows.shape
    if features % (count * HEAD_DIM) or tokens % FIRST_ROWS or tokens == FIRST_ROWS:
        attention_out = gathered_attention(query_rows, key_rows, value_rows, out_weight)
        return (hyena(hyena_query, hyena_key, hyena_value, conv_filter, skip_gain), attention_out)
    attended, keys, values, queries = first_attention(query_rows, key_rows, value_rows, count)
    first_part = project(out_weight, attended)
    first_part, keys, values, queries = lax.optimization_barrier(
        (first_part, keys, values, queries)
    )
    first_sum = summed(first_part)
    later_part = project(out_weight, later_attention(queries, keys, values))
    later_part, hyena_query, hyena_key, hyena_value = lax.optimization_barrier(
        (later_part, hyena_query, hyena_key, hyena_value)
    )
    later_sum = summed(later_part)
    hyena_out = hyena(hyena_query, hyena_key, hyena_value, conv_filter, skip_gain)
    return (hyena_out, jnp.concatenate([first_sum, later_sum], axis=1))


def solution(mesh):
    in_specs = (
        P("ctx", "tp"),
        P("ctx", "tp"),
        P("ctx", "tp"),
        P("tp", None),
        P("tp"),
        P("ctx", "tp"),
        P("ctx", "tp"),
        P("ctx", "tp"),
        P(None, "tp"),
    )
    out_specs = (P("ctx", "tp"), P("tp", "ctx"))
    return jax.shard_map(local, mesh=mesh, in_specs=in_specs, out_specs=out_specs, check_vma=False)
```

```python
import functools

import jax
import jax.numpy as jnp
from jax import lax
from jax.experimental import pallas as pl
from jax.experimental.pallas import tpu as pltpu
from jax.sharding import PartitionSpec as P

HEAD_DIM = 128
FIRST_ROWS = 128
EXP_SCALE = HEAD_DIM ** (-0.5) * 1.4426950408889634
MESH = pl.DeviceIdType.MESH
ANY = pl.BlockSpec(memory_space=pl.ANY)


def greet(count, me):
    barrier = pltpu.get_barrier_semaphore()
    for offset in range(1, count):
        peer = lax.rem(me + offset, count)
        pl.semaphore_signal(barrier, inc=1, device_id={"ctx": peer}, device_id_type=MESH)
    pl.semaphore_wait(barrier, count - 1)


def attend(queries, keys, values, known, column):
    rows = queries.shape[0]
    contract = (((1,), (1,)), ((), ()))
    diagonal = keys[pl.ds(known, rows), pl.ds(column, HEAD_DIM)]
    scores = lax.dot_general(queries, diagonal, contract, preferred_element_type=jnp.float32)
    allowed = lax.broadcasted_iota(jnp.int32, (rows, rows), 1) <= lax.broadcasted_iota(
        jnp.int32, (rows, rows), 0
    )
    scores = jnp.where(allowed, scores, -jnp.inf)
    top = jnp.max(scores, axis=1, keepdims=True)
    if known:
        early = lax.dot_general(
            queries,
            keys[pl.ds(0, known), pl.ds(column, HEAD_DIM)],
            contract,
            preferred_element_type=jnp.float32,
        )
        top = jnp.maximum(top, jnp.max(early, axis=1, keepdims=True))
    weights = jnp.exp2((scores - top) * EXP_SCALE)
    total = jnp.sum(weights, axis=1, keepdims=True)
    mixed = jnp.dot(
        weights.astype(jnp.bfloat16),
        values[pl.ds(known, rows), pl.ds(column, HEAD_DIM)],
        preferred_element_type=jnp.float32,
    )
    if known:
        weights = jnp.exp2((early - top) * EXP_SCALE)
        total = total + jnp.sum(weights, axis=1, keepdims=True)
        mixed = mixed + jnp.dot(
            weights.astype(jnp.bfloat16),
            values[pl.ds(0, known), pl.ds(column, HEAD_DIM)],
            preferred_element_type=jnp.float32,
        )
    return (mixed / total).astype(jnp.bfloat16)


def give_back(block, me, width, done, attended, send_sem, recv_sem, local_sem):
    column = pl.multiple_of(me * width, width)
    target = attended.at[:, pl.ds(column, width)]

    @pl.when(me != block)
    def _():
        pltpu.make_async_remote_copy(
            src_ref=done.at[block],
            dst_ref=target,
            send_sem=send_sem.at[block],
            recv_sem=recv_sem.at[me],
            device_id={"ctx": block},
            device_id_type=MESH,
        ).start()

    @pl.when(me == block)
    def _():
        pltpu.make_async_copy(done.at[block], target, local_sem).start()


def end_back(count, me, width, done, attended, send_sem, recv_sem, local_sem):
    for block in range(count):
        column = block * width
        target = attended.at[:, pl.ds(column, width)]

        @pl.when(me != block)
        def _():
            copy = pltpu.make_async_remote_copy(
                src_ref=done.at[block],
                dst_ref=target,
                send_sem=send_sem.at[block],
                recv_sem=recv_sem.at[block],
                device_id={"ctx": block},
                device_id_type=MESH,
            )
            copy.wait_send()
            copy.wait_recv()

        @pl.when(me == block)
        def _():
            pltpu.make_async_copy(done.at[block], target, local_sem).wait()


def first_kernel(
    count,
    query,
    key,
    value,
    attended,
    key_out,
    value_out,
    late_out,
    keys,
    values,
    early,
    done,
    send_sem,
    recv_sem,
    own_sem,
    back_send,
    back_recv,
    back_local,
    out_sem,
):
    me = lax.axis_index("ctx")
    tokens = key.shape[0]
    width = key.shape[1] // count
    first = early.shape[1]
    late = tokens - first

    def pieces(source, reader):
        column = pl.multiple_of(reader * width, width)
        columns = pl.ds(column, width)
        rows = pl.ds(pl.multiple_of(source * tokens, tokens), tokens)
        return (
            (key.at[:, columns], keys.at[rows]),
            (value.at[:, columns], values.at[rows]),
            (query.at[pl.ds(0, first), columns], early.at[source]),
            (query.at[pl.ds(first, late), columns], late_out.at[source]),
        )

    def sent(kind, source, reader, other):
        origin, target = pieces(source, reader)[kind]
        return pltpu.make_async_remote_copy(
            src_ref=origin,
            dst_ref=target,
            send_sem=send_sem.at[kind, reader],
            recv_sem=recv_sem.at[kind, source],
            device_id={"ctx": other},
            device_id_type=MESH,
        )

    def own(kind):
        origin, target = pieces(me, me)[kind]
        return pltpu.make_async_copy(origin, target, own_sem.at[kind])

    greet(count, me)
    for kind in range(4):
        for offset in range(1, count):
            peer = lax.rem(me + offset, count)
            sent(kind, me, peer, peer).start()
        own(kind).start()
    for block in range(count):

        @pl.when(me != block)
        def _():
            for kind in range(3):
                sent(kind, block, me, block).wait_recv()

        @pl.when(me == block)
        def _():
            for kind in range(3):
                own(kind).wait()

        @pl.loop(0, width // HEAD_DIM)
        def _(head):
            column = pl.multiple_of(head * HEAD_DIM, HEAD_DIM)
            done[block, :, pl.ds(column, HEAD_DIM)] = attend(
                early[block, :, pl.ds(column, HEAD_DIM)], keys, values, block * tokens, column
            )

        give_back(block, me, width, done, attended, back_send, back_recv, back_local)
    saved = (
        pltpu.make_async_copy(keys, key_out, out_sem.at[0]),
        pltpu.make_async_copy(values, value_out, out_sem.at[1]),
    )
    for copy in saved:
        copy.start()
    end_back(count, me, width, done, attended, back_send, back_recv, back_local)
    for offset in range(1, count):
        peer = lax.rem(me + offset, count)
        sent(3, peer, me, peer).wait_recv()
        for kind in range(4):
            sent(kind, me, peer, peer).wait_send()
    own(3).wait()
    for copy in saved:
        copy.wait()


def later_kernel(
    count, query, keys, values, attended, done, back_send, back_recv, back_local
):
    me = lax.axis_index("ctx")
    width = keys.shape[1]
    tokens = keys.shape[0] // count
    late = query.shape[1]
    greet(count, me)
    for block in range(count):
        for start in range(0, late, FIRST_ROWS):

            @pl.loop(0, width // HEAD_DIM)
            def _(head):
                column = pl.multiple_of(head * HEAD_DIM, HEAD_DIM)
                columns = pl.ds(column, HEAD_DIM)
                rows = pl.ds(start, FIRST_ROWS)
                known = block * tokens + (tokens - late) + start
                done[block, rows, columns] = attend(
                    query[block, rows, columns], keys, values, known, column
                )

        give_back(block, me, width, done, attended, back_send, back_recv, back_local)
    end_back(count, me, width, done, attended, back_send, back_recv, back_local)


def first_attention(query, key, value, count):
    tokens, features = key.shape
    width = features // count
    late = tokens - FIRST_ROWS
    kind = jnp.bfloat16
    return pl.pallas_call(
        functools.partial(first_kernel, count),
        out_shape=(
            jax.ShapeDtypeStruct((FIRST_ROWS, features), kind),
            jax.ShapeDtypeStruct((count * tokens, width), kind),
            jax.ShapeDtypeStruct((count * tokens, width), kind),
            jax.ShapeDtypeStruct((count, late, width), kind),
        ),
        in_specs=[ANY] * 3,
        out_specs=(ANY,) * 4,
        scratch_shapes=[
            pltpu.VMEM((count * tokens, width), kind),
            pltpu.VMEM((count * tokens, width), kind),
            pltpu.VMEM((count, FIRST_ROWS, width), kind),
            pltpu.VMEM((count, FIRST_ROWS, width), kind),
            pltpu.SemaphoreType.DMA((4, count)),
            pltpu.SemaphoreType.DMA((4, count)),
            pltpu.SemaphoreType.DMA((4,)),
            pltpu.SemaphoreType.DMA((count,)),
            pltpu.SemaphoreType.DMA((count,)),
            pltpu.SemaphoreType.DMA,
            pltpu.SemaphoreType.DMA((2,)),
        ],
        compiler_params=pltpu.CompilerParams(
            collective_id=0, has_side_effects=True, vmem_limit_bytes=40 << 20
        ),
    )(query, key, value)


def later_attention(query, keys, values):
    count, late, width = query.shape
    kind = jnp.bfloat16
    return pl.pallas_call(
        functools.partial(later_kernel, count),
        out_shape=jax.ShapeDtypeStruct((late, count * width), kind),
        in_specs=[pl.BlockSpec(memory_space=pltpu.VMEM)] * 3,
        out_specs=ANY,
        scratch_shapes=[
            pltpu.VMEM((count, late, width), kind),
            pltpu.SemaphoreType.DMA((count,)),
            pltpu.SemaphoreType.DMA((count,)),
            pltpu.SemaphoreType.DMA,
        ],
        compiler_params=pltpu.CompilerParams(
            collective_id=1, has_side_effects=True, vmem_limit_bytes=40 << 20
        ),
    )(query, keys, values)


def project_kernel(weight, attended, out):
    out[...] = lax.dot_general(
        weight[...],
        attended[...],
        (((1,), (1,)), ((), ())),
        preferred_element_type=jnp.float32,
    ).astype(out.dtype)


def project(weight, attended, part=0, parts=1):
    outs, features = weight.shape
    tokens = attended.shape[0]
    step = 512
    steps = outs // lax.axis_size("tp") // parts // step
    outs = outs // parts
    return pl.pallas_call(
        project_kernel,
        grid=(outs // step,),
        out_shape=jax.ShapeDtypeStruct((outs, tokens), jnp.bfloat16),
        in_specs=[
            pl.BlockSpec(
                (step, features),
                lambda i: ((i // steps) * (steps * parts) + part * steps + i % steps, 0),
            ),
            pl.BlockSpec((tokens, features), lambda i: (0, 0)),
        ],
        out_specs=pl.BlockSpec((step, tokens), lambda i: (i, 0)),
        compiler_params=pltpu.CompilerParams(vmem_limit_bytes=40 << 20),
        cost_estimate=pl.CostEstimate(
            flops=2 * outs * tokens * features,
            bytes_accessed=2 * outs * features,
            transcendentals=0,
        ),
    )(weight, attended)


def summed(partial):
    return lax.psum_scatter(partial, "tp", scatter_dimension=0, tiled=True)


def shifted(block, axis, distance):
    devices = range(lax.axis_size(axis))
    route = [(i - distance, i) for i in devices if i - distance in devices]
    return lax.ppermute(block, axis, route)


def swapped(block, axis, stride):
    count = lax.axis_size(axis)
    route = []
    for low in range(count):
        high = low | 1 << stride
        if high != low and high < count:
            route += [(low, high), (high, low)]
    return lax.ppermute(block, axis, route)


def toeplitz_pair(filters):
    length = filters.shape[1]
    lag_table = (
        jnp.arange(length, dtype=jnp.int32)[:, None] - jnp.arange(length, dtype=jnp.int32)[None, :]
    )
    taps = jnp.arange(length, dtype=jnp.int32)[:, None, None]
    inner_table = (lag_table[None] == taps).astype(jnp.bfloat16)
    outer_table = (lag_table[None] + length == taps).astype(jnp.bfloat16)
    inner_part = jnp.einsum(
        "gj,jts->gts", filters, inner_table, preferred_element_type=jnp.float32
    ).astype(jnp.bfloat16)
    outer_part = jnp.einsum(
        "gj,jts->gts", filters, outer_table, preferred_element_type=jnp.float32
    ).astype(jnp.bfloat16)
    return (inner_part, outer_part)


def local_conv(current, before, filters):
    blocks, length, feature_width = current.shape
    groups = filters.shape[0]
    split_shape = (blocks, length, groups, feature_width // groups)
    inner_part, outer_part = toeplitz_pair(filters)
    result = jnp.einsum(
        "gts,bsgc->btgc",
        inner_part,
        current.reshape(split_shape),
        preferred_element_type=jnp.float32,
    )
    result = result + jnp.einsum(
        "gts,bsgc->btgc",
        outer_part,
        before.reshape(split_shape),
        preferred_element_type=jnp.float32,
    )
    return result.reshape(blocks * length, feature_width)


def half_update(partial_value, block_keys, block_values, block_first, queries, positions):
    row_top, row_total, weighted = partial_value
    score_scale = HEAD_DIM ** (-0.5)
    scores = (
        jnp.einsum("qhd,khd->hqk", queries, block_keys, preferred_element_type=jnp.float32)
        * score_scale
    )
    key_positions = block_first + jnp.arange(block_keys.shape[0], dtype=jnp.int32)
    allowed = key_positions[None, :] <= positions[:, None]
    scores = jnp.where(allowed[None], scores, -jnp.inf)
    new_top = jnp.maximum(row_top, jnp.max(scores, axis=2))
    safe_top = jnp.where(new_top == -jnp.inf, 0.0, new_top)
    keep_factor = jnp.exp(row_top - safe_top)
    weights = jnp.exp(scores - safe_top[:, :, None])
    row_total = row_total * keep_factor + jnp.sum(weights, axis=2)
    weighted = weighted * keep_factor[:, :, None] + jnp.einsum(
        "hqk,khd->hqd",
        weights.astype(jnp.bfloat16),
        block_values,
        preferred_element_type=jnp.float32,
    )
    return (new_top, row_total, weighted)


def hyena(hyena_query, hyena_key, hyena_value, conv_filter, skip_gain):
    product = (hyena_key.astype(jnp.float32) * hyena_value.astype(jnp.float32)).astype(jnp.bfloat16)
    length = conv_filter.shape[1]
    tokens_here, feature_width = product.shape
    blocks = tokens_here // length
    previous = shifted(product[tokens_here - length :], "ctx", 1)
    widened = product.astype(jnp.float32)
    earlier = jnp.concatenate([previous, product[: tokens_here - length]], axis=0)
    convolved = local_conv(
        product.reshape(blocks, length, feature_width),
        earlier.reshape(blocks, length, feature_width),
        conv_filter,
    )
    hyena_out = (
        hyena_query.astype(jnp.float32) * (convolved + skip_gain[None, :] * widened)
    ).astype(jnp.bfloat16)
    return hyena_out


def gathered_attention(query_rows, key_rows, value_rows, out_weight):
    tokens_here, feature_width = key_rows.shape
    ctx_count = lax.axis_size("ctx")
    ctx_index = lax.axis_index("ctx")
    half_rows = tokens_here // 2
    heads_here = feature_width // HEAD_DIM
    offsets = jnp.arange(half_rows, dtype=jnp.int32)
    first_positions = ctx_index * tokens_here + offsets
    second_queries = query_rows[half_rows:]
    for bit_index in range(ctx_count.bit_length() - 1):
        second_queries = swapped(second_queries, "ctx", bit_index)
    second_positions = (ctx_count - 1 - ctx_index) * tokens_here + half_rows + offsets
    query_halves = (
        query_rows[:half_rows].reshape(half_rows, heads_here, HEAD_DIM),
        second_queries.reshape(half_rows, heads_here, HEAD_DIM),
    )
    position_halves = (first_positions, second_positions)
    empty_top = jnp.full((heads_here, half_rows), -jnp.inf, jnp.float32)
    empty_total = jnp.zeros((heads_here, half_rows), jnp.float32)
    empty_weighted = jnp.zeros((heads_here, half_rows, HEAD_DIM), jnp.float32)
    start_state = (
        (empty_top, empty_total, empty_weighted),
        (empty_top, empty_total, empty_weighted),
    )
    key_piece = lax.all_gather(key_rows, "ctx", axis=0, tiled=True)
    value_piece = lax.all_gather(value_rows, "ctx", axis=0, tiled=True)
    piece_rows = key_piece.shape[0]
    step_rows = min(piece_rows, tokens_here)
    count_steps = piece_rows // step_rows
    key_steps = key_piece.reshape(count_steps, step_rows, heads_here, HEAD_DIM)
    value_steps = value_piece.reshape(count_steps, step_rows, heads_here, HEAD_DIM)

    def one_step(carried, inputs):
        block_keys, block_values, step_index = inputs
        block_first = step_index * step_rows
        updated = []
        for half_index in range(2):
            queries = query_halves[half_index]
            positions = position_halves[half_index]

            def apply_update(partial_value, queries=queries, positions=positions):
                return half_update(
                    partial_value, block_keys, block_values, block_first, queries, positions
                )

            def leave_alone(partial_value):
                return partial_value

            updated.append(
                lax.cond(
                    block_first <= positions[half_rows - 1],
                    apply_update,
                    leave_alone,
                    carried[half_index],
                )
            )
        return ((updated[0], updated[1]), None)

    final_state, unused = lax.scan(
        one_step, start_state, (key_steps, value_steps, jnp.arange(count_steps, dtype=jnp.int32))
    )
    first_state, second_state = final_state

    def finish(partial_value):
        row_top, row_total, weighted = partial_value
        normalized = weighted / row_total[:, :, None]
        return (
            jnp.transpose(normalized, (1, 0, 2))
            .reshape(half_rows, feature_width)
            .astype(jnp.bfloat16)
        )

    first_result = finish(first_state)
    second_result = finish(second_state)
    for bit_index in range(ctx_count.bit_length() - 1):
        second_result = swapped(second_result, "ctx", bit_index)
    attended = jnp.concatenate([first_result, second_result], axis=0)
    attention_out = lax.psum_scatter(
        lax.dot_general(
            out_weight, attended, (((1,), (1,)), ((), ())), preferred_element_type=jnp.float32
        ).astype(jnp.bfloat16),
        "tp",
        scatter_dimension=0,
        tiled=True,
    )
    return attention_out


def local(
    hyena_query,
    hyena_key,
    hyena_value,
    conv_filter,
    skip_gain,
    query_rows,
    key_rows,
    value_rows,
    out_weight,
):
    count = lax.axis_size("ctx")
    tokens, features = key_rows.shape
    if features % (count * HEAD_DIM) or tokens % FIRST_ROWS or tokens == FIRST_ROWS:
        attention_out = gathered_attention(query_rows, key_rows, value_rows, out_weight)
        return (hyena(hyena_query, hyena_key, hyena_value, conv_filter, skip_gain), attention_out)
    attended, keys, values, queries = first_attention(query_rows, key_rows, value_rows, count)
    first_part = project(out_weight, attended)
    first_part, keys, values, queries = lax.optimization_barrier(
        (first_part, keys, values, queries)
    )
    first_sum = summed(first_part)
    attended = later_attention(queries, keys, values)
    upper_part = project(out_weight, attended, 0, 2)
    upper_part, attended = lax.optimization_barrier((upper_part, attended))
    upper_sum = summed(upper_part)
    lower_part = project(out_weight, attended, 1, 2)
    lower_part, hyena_query, hyena_key, hyena_value = lax.optimization_barrier(
        (lower_part, hyena_query, hyena_key, hyena_value)
    )
    later_sum = jnp.concatenate([upper_sum, summed(lower_part)], axis=0)
    hyena_out = hyena(hyena_query, hyena_key, hyena_value, conv_filter, skip_gain)
    return (hyena_out, jnp.concatenate([first_sum, later_sum], axis=1))


def solution(mesh):
    in_specs = (
        P("ctx", "tp"),
        P("ctx", "tp"),
        P("ctx", "tp"),
        P("tp", None),
        P("tp"),
        P("ctx", "tp"),
        P("ctx", "tp"),
        P("ctx", "tp"),
        P(None, "tp"),
    )
    out_specs = (P("ctx", "tp"), P("tp", "ctx"))
    return jax.shard_map(local, mesh=mesh, in_specs=in_specs, out_specs=out_specs, check_vma=False)
```
